32 devices in a mesh: pipe: 4 (over z), hid: 8 (over y, x, core).
Axes of the slice: x: 2, y: 2, z: 4, core: 2. Of those that a mesh axis runs over, the one named last changes fastest.
Arguments:
- section_inputs: bfloat16 [4, 3, 256, 1024], P('pipe', None, 'hid'), may hold values from -6 to 6
- w_in: bfloat16 [4, 1024, 32768], P('pipe', None, 'hid'), may hold values from -0.1875 to 0.1875
- w_out: bfloat16 [4, 32768, 1024], P('pipe', 'hid'), may hold values from -0.03125 to 0.03125
- warm_factor: float32 [4, 1024, 16], P('pipe'), may hold values from -6 to 6
- pending_left: float32 [4, 256, 16], P('pipe'), may hold values from -0.375 to 0.375
- pending_right: float32 [4, 1024, 16], P('pipe'), may hold values from -24 to 24
- incoming_left: float32 [3, 256, 16], replicated, may hold values from -0.375 to 0.375
- incoming_right: float32 [3, 1024, 16], replicated, may hold values from -24 to 24
Outputs:
- section_grads: float32 [4, 256, 1024], P('pipe', 'hid')
- final_left: float32 [4, 256, 16], P('pipe', 'hid')
- final_right: float32 [4, 1024, 16], P('pipe')
The draws below stay inside these ranges and needn't reach their ends.
All inputs are finite; a program needn't handle non-finite values.
Results may differ from the reference program's by a relative error of at most 0.02.
Values may be sent and summed in bfloat16 or wider, within the bound.
No kernel may reach another device: no remote copies, remote signals or barrier semaphores. Data moves between devices by JAX's collectives and lax.ppermute only.
A program may use at most 64 MiB of HBM per device.

```python
import jax
import jax.numpy as jnp
from jax import lax

D = 1024
FF = 32768
RANK = 16
TICKS = 3
ROWS = 256
SECTIONS = 4


def factor_entries(key, shape, scale):
    values = jax.random.truncated_normal(key, -6.0, 6.0, shape, jnp.float32)
    return values * scale


def draw_warm_factor(key, part):
    return factor_entries(jax.random.fold_in(key, 11), (SECTIONS, D, RANK), 1.0)


def draw_pending_left(key, part):
    return factor_entries(jax.random.fold_in(key, 12), (SECTIONS, ROWS, RANK), 0.0625)


def draw_pending_right(key, part):
    return factor_entries(jax.random.fold_in(key, 13), (SECTIONS, D, RANK), 4.0)


def draw_incoming_left(key, part):
    return factor_entries(jax.random.fold_in(key, 14), (TICKS, ROWS, RANK), 0.0625)


def draw_incoming_right(key, part):
    return factor_entries(jax.random.fold_in(key, 15), (TICKS, D, RANK), 4.0)


def block_scale(stream_key, shape, shards, smallest, largest):
    level, own = 1.0, jax.random.fold_in(stream_key, 6)
    for position, parts in shards:
        steps = jnp.exp(jax.random.uniform(jax.random.fold_in(own, position), (parts,), jnp.float32, smallest / len(shards), largest / len(shards)))
        level = level * jnp.repeat(steps, shape[position] // parts).reshape([-1 if axis == position else 1 for axis in range(len(shape))])
    return level


def noise(stream_key, dims, scale, reach, split=(), kind=jnp.bfloat16):
    result = scale * jax.random.normal(stream_key, dims, jnp.float32)
    if split:
        result = result * block_scale(stream_key, dims, split, -0.22, 0.18)
    return jnp.clip(result, -reach, reach).astype(kind)


def setup_inputs(seed: int = 0) -> dict:
    key_list = jax.random.split(jax.random.key(seed), 9)
    return {
        "section_inputs": noise(key_list[0], (SECTIONS, TICKS, ROWS, D), 1.0, 6.0, ((0, 4), (2, 8))),
        "w_in": noise(key_list[1], (SECTIONS, D, FF), D ** -0.5, 0.1875, ((0, 4), (2, 8))),
        "w_out": noise(key_list[2], (SECTIONS, FF, D), FF ** -0.5, 0.03125, ((0, 4), (1, 8))),
        "warm_factor": draw_warm_factor(jax.random.fold_in(key_list[8], 71), 0),
        "pending_left": draw_pending_left(jax.random.fold_in(key_list[8], 71), 0),
        "pending_right": draw_pending_right(jax.random.fold_in(key_list[8], 71), 0),
        "incoming_left": draw_incoming_left(jax.random.fold_in(key_list[8], 71), 0),
        "incoming_right": draw_incoming_right(jax.random.fold_in(key_list[8], 71), 0),
    }


def orthonormal(merged, warm_basis):
    projected = jnp.dot(merged.astype(jnp.float32), warm_basis.astype(jnp.float32), precision=lax.Precision.HIGHEST, preferred_element_type=jnp.float32)
    gram_matrix = jnp.dot(projected.T.astype(jnp.float32), projected.astype(jnp.float32), precision=lax.Precision.HIGHEST, preferred_element_type=jnp.float32)
    lower_factor = jnp.linalg.cholesky(gram_matrix)
    new_left = jax.scipy.linalg.solve_triangular(lower_factor, projected.T, lower=True).T
    new_right = jnp.dot(merged.T.astype(jnp.float32), new_left.astype(jnp.float32), precision=lax.Precision.HIGHEST, preferred_element_type=jnp.float32)
    return (new_left, new_right)

def per_section(section_items):
    inputs_now, w_in_section, w_out_section, left_factor, right_factor, warm_basis = section_items
    cotangent = jnp.dot(left_factor.astype(jnp.float32), right_factor.T.astype(jnp.float32), precision=lax.Precision.HIGHEST, preferred_element_type=jnp.float32)
    cotangent_low = cotangent.astype(jnp.bfloat16)
    upward = jnp.dot(cotangent_low.astype(jnp.float32), w_out_section.T.astype(jnp.float32), preferred_element_type=jnp.float32)
    preact = jnp.dot(inputs_now.astype(jnp.float32), w_in_section.astype(jnp.float32), preferred_element_type=jnp.float32)
    hidden_grad = jnp.where(preact > 0, upward, jnp.zeros_like(upward)).astype(jnp.bfloat16)
    merged = cotangent + jnp.dot(hidden_grad.astype(jnp.float32), w_in_section.T.astype(jnp.float32), preferred_element_type=jnp.float32)
    new_left, new_right = orthonormal(merged, warm_basis)
    return (merged, new_left, new_right)

def reference(section_inputs, w_in, w_out, warm_factor, pending_left, pending_right, incoming_left, incoming_right):
    held_left = pending_left
    held_right = pending_right
    warm_basis = warm_factor
    merged = None
    new_left = None
    new_right = None
    for tick_index in range(TICKS):
        left_all = jnp.concatenate([held_left[:-1], incoming_left[tick_index][None]], 0)
        right_all = jnp.concatenate([held_right[:-1], incoming_right[tick_index][None]], 0)
        merged, new_left, new_right = lax.map(per_section, (section_inputs[:, tick_index], w_in, w_out, left_all, right_all, warm_basis))
        held_left = jnp.concatenate([new_left[1:], jnp.zeros_like(new_left[:1])], 0)
        held_right = jnp.concatenate([new_right[1:], jnp.zeros_like(new_right[:1])], 0)
        warm_basis = new_right
    return (merged, new_left, new_right)
```

```python
import functools

import jax
import jax.numpy as jnp
from jax import lax
from jax.experimental import pallas as pl
from jax.experimental.pallas import tpu as pltpu
from jax.sharding import PartitionSpec as P

F32 = jnp.float32
BF16 = jnp.bfloat16
HIGH = lax.Precision.HIGHEST
VMEM = pl.BlockSpec(memory_space=pltpu.VMEM)
SMEM = pl.BlockSpec(memory_space=pltpu.SMEM)
LIMIT = 8 << 20


def dot(first, second, first_dim, second_dim, precision=None):
    return lax.dot_general(
        first,
        second,
        (((first_dim,), (second_dim,)), ((), ())),
        precision=precision,
        preferred_element_type=F32,
    )


def split(value):
    high = value.astype(BF16)
    low = (value - high.astype(F32)).astype(BF16)
    return jnp.concatenate([high, low], 0)


def chunks(total):
    size = min(total, 1024)
    return [(start, size) for start in range(0, total, size)]


def cotangent_of(left_t, right_t):
    rank = left_t.shape[0]
    lefts, rights = split(left_t), split(right_t)
    first = jnp.concatenate([lefts[:rank], lefts], 0)
    second = jnp.concatenate([rights, rights[:rank]], 0)
    return dot(first, second, 0, 0)


def chosen(place_ref, incoming, other):
    return jnp.where(place_ref[1] == 1, incoming, other)


def on_device(kernel, outs, operands, flops, name, smem=0, scratch=()):
    many = isinstance(outs, list)
    shapes = [jax.ShapeDtypeStruct(*out) for out in (outs if many else [outs])]
    moved = sum(o.size * o.dtype.itemsize for o in operands)
    result = pl.pallas_call(
        kernel,
        out_shape=shapes,
        in_specs=[SMEM] * smem + [VMEM] * (len(operands) - smem),
        out_specs=[VMEM] * len(shapes),
        scratch_shapes=list(scratch),
        compiler_params=pltpu.CompilerParams(vmem_limit_bytes=LIMIT),
        cost_estimate=pl.CostEstimate(
            flops=flops, bytes_accessed=moved // 4, transcendentals=0
        ),
        name=name,
    )(*operands)
    return result if many else result[0]


def up_kernel(place_ref, in_left_ref, in_right_ref, left_ref, right_ref, w_out_ref, up_ref, left_out, right_out):
    left = chosen(place_ref, in_left_ref[0], left_ref[...])
    right = chosen(place_ref, in_right_ref[0], right_ref[...])
    left_out[...] = left
    right_out[...] = right
    cotangent_low = cotangent_of(left, right).astype(BF16)
    for start, size in chunks(w_out_ref.shape[0]):
        up_ref[:, start : start + size] = dot(
            cotangent_low, w_out_ref[start : start + size, :], 1, 1
        ).astype(BF16)


def warm_kernel(warm_ref, w_in_ref, out_ref):
    stacked = split(warm_ref[...])
    rank = warm_ref.shape[0]
    for start, size in chunks(w_in_ref.shape[1]):
        both = dot(stacked, w_in_ref[:, start : start + size], 1, 0)
        out_ref[:, start : start + size] = split(both[:rank] + both[rank:])


def own_term(place_ref, left, right, warm):
    inner = dot(warm, right, 1, 1, HIGH)
    return jnp.where(place_ref[0] == 0, 1.0, 0.0) * dot(inner, left, 1, 0, HIGH)


def place_rows(offsets, place_ref, pieces, rows_ref):
    block = pieces[0].shape[0]
    for offset, piece in zip(offsets, pieces):
        place = 0
        if len(pieces) > 1:
            place = pl.multiple_of(jnp.bitwise_xor(place_ref[0], offset) * block, block)
        rows_ref[pl.ds(place, block), :] = piece[...]


def first_kernel(offsets, place_ref, *refs):
    pieces, rest = refs[: len(offsets)], refs[len(offsets) :]
    w_in_ref, up_ref, warm_in_ref, left_ref, right_ref, warm_ref, hidden_ref, proj_ref, rows_ref = rest
    place_rows(offsets, place_ref, pieces, rows_ref)
    rank = left_ref.shape[0]
    total = None
    for start, size in chunks(w_in_ref.shape[1]):
        preact = dot(rows_ref[...], w_in_ref[:, start : start + size], 1, 0)
        up = up_ref[:, start : start + size]
        hidden = jnp.where(preact > 0, up.astype(F32), 0.0).astype(BF16)
        hidden_ref[:, start : start + size] = hidden
        part = dot(hidden, warm_in_ref[:, start : start + size], 1, 1)
        total = part if total is None else total + part
    turned = total.T
    proj_ref[...] = (
        turned[:rank] + turned[rank:] + own_term(place_ref, left_ref[...], right_ref[...], warm_ref[...])
    )


def mask_kernel(offsets, step, place_ref, *refs):
    pieces, (w_in_ref, mask_ref, rows_ref) = refs[: len(offsets)], refs[len(offsets) :]
    place_rows(offsets, place_ref, [piece.at[step] for piece in pieces], rows_ref)
    for start, size in chunks(w_in_ref.shape[1]):
        preact = dot(rows_ref[...], w_in_ref[:, start : start + size], 1, 0)
        mask_ref[:, start : start + size] = jnp.where(preact > 0, 1.0, 0.0).astype(BF16)


def hidden_kernel(
    tick, place_ref, in_left_ref, in_right_ref, both_ref, warm_ref, w_out_ref, mask_ref, warm_in_ref,
    hidden_ref, proj_ref, left_out, right_out,
):
    rank, rows = left_out.shape
    left = chosen(place_ref, in_left_ref[tick], both_ref[:, :rows])
    right = chosen(place_ref, in_right_ref[tick], both_ref[:, rows:])
    left_out[...] = left
    right_out[...] = right
    cotangent_low = cotangent_of(left, right).astype(BF16)
    total = None
    for start, size in chunks(w_out_ref.shape[0]):
        up = dot(cotangent_low, w_out_ref[start : start + size, :], 1, 1)
        mask = mask_ref[:, start : start + size]
        hidden = jnp.where(mask.astype(F32) > 0, up, 0.0).astype(BF16)
        hidden_ref[:, start : start + size] = hidden
        part = dot(hidden, warm_in_ref[:, start : start + size], 1, 1)
        total = part if total is None else total + part
    turned = total.T
    proj_ref[...] = turned[:rank] + turned[rank:] + own_term(place_ref, left, right, warm_ref[...])


def merged_kernel(place_ref, left_ref, right_ref, hidden_ref, w_in_ref, merged_ref):
    share = jnp.where(place_ref[0] == 0, 1.0, 0.0)
    depth = w_in_ref.shape[0]
    size = min(depth, 256)
    for start in range(0, depth, size):
        here = slice(start, start + size)
        merged_ref[:, here] = dot(hidden_ref[...], w_in_ref[here, :], 1, 1) + share * cotangent_of(
            left_ref[...], right_ref[:, here]
        )


def right_kernel(proj_ref, merged_ref, out_ref):
    stacked = split(proj_ref[...])
    rank = proj_ref.shape[0]
    merged = merged_ref[...]
    high = merged.astype(BF16)
    low = (merged - high.astype(F32)).astype(BF16)
    both = dot(stacked, high, 1, 0) + dot(stacked, low, 1, 0)
    out_ref[...] = both[:rank] + both[rank:]


def factor_kernel(proj_ref, left_ref, inverse_ref):
    proj = proj_ref[...]
    rank = proj.shape[0]
    gram = dot(proj, proj, 1, 1, HIGH)
    line = lax.broadcasted_iota(jnp.int32, (rank, rank), 0)
    column = lax.broadcasted_iota(jnp.int32, (rank, rank), 1)
    eye = jnp.where(line == column, 1.0, 0.0)
    inverse = eye
    for step in range(rank):
        pivot_row = gram[step : step + 1, :]
        pivot = gram[step : step + 1, step : step + 1]
        scale = jnp.where(line[:, :1] > step, gram[:, step : step + 1] / pivot, 0.0)
        inverse = inverse - scale * inverse[step : step + 1, :]
        gram = gram - scale * pivot_row
    pivots = jnp.sum(gram * eye, axis=1, keepdims=True)
    inverse = inverse * lax.rsqrt(pivots)
    inverse_ref[...] = inverse
    left_ref[...] = dot(inverse, proj, 1, 0, HIGH)


def finish_kernel(inverse_ref, left_ref, sums_ref, right_ref, both_ref):
    right = dot(inverse_ref[...], sums_ref[...], 1, 0, HIGH)
    rows = left_ref.shape[1]
    right_ref[...] = right
    both_ref[:, :rows] = left_ref[...]
    both_ref[:, rows:] = right


def outgoing_kernel(place_ref, merged_ref, out_ref):
    block = out_ref.shape[1]
    for chip in range(out_ref.shape[0]):
        start = pl.multiple_of((2 * chip + 1 - place_ref[0] % 2) * block, block)
        out_ref[chip] = merged_ref[pl.ds(start, block), :].astype(BF16)


def pack_kernel(chips, place_ref, merged_ref, arrived_ref, right_ref, right_arrived_ref, own_ref, right_out, *out_refs):
    block = own_ref.shape[0]
    core, chip = place_ref[0] % 2, place_ref[0] // 2
    stacked = split(right_ref[...] + right_arrived_ref[...])
    rank = right_ref.shape[0]
    right_out[...] = stacked[:rank].astype(F32) + stacked[rank:].astype(F32)
    for turn in range(chips):
        target = jnp.bitwise_xor(chip, turn)
        start = pl.multiple_of((2 * target + core) * block, block)
        value = merged_ref[pl.ds(start, block), :] + arrived_ref[target].astype(F32)
        if turn:
            out_refs[turn - 1][:block, :] = value.astype(BF16)
            out_refs[turn - 1][block:, :] = stacked
        else:
            own_ref[...] = value


def last_kernel(inverse_ref, own_ref, right_own_ref, *refs):
    packs, (grads_ref, right_ref) = refs[:-2], refs[-2:]
    block, rank = own_ref.shape[0], inverse_ref.shape[0]
    rows = [own_ref[...]] + [pack[:block, :].astype(F32) for pack in packs]
    sums = [right_own_ref[...]] + [
        pack[block : block + rank, :].astype(F32) + pack[block + rank :, :].astype(F32) for pack in packs
    ]
    grads_ref[...] = tree_sum(rows)
    right_ref[...] = dot(inverse_ref[...], tree_sum(sums), 1, 0, HIGH)


def flip(value, axis, bits):
    count = lax.axis_size(axis)
    return lax.ppermute(value, axis, [(source, source ^ bits) for source in range(count)])


def stages(count):
    found, stride = [], 1
    while stride < count:
        members = 2 if stride == 1 else min(4, count // stride)
        found.append((stride, members))
        stride *= members
    return found


def tree_sum(parts):
    while len(parts) > 1:
        parts = [first + second for first, second in zip(parts[::2], parts[1::2])]
    return parts[0]


def all_sum(value):
    for stride, members in stages(lax.axis_size("hid")):
        value = tree_sum([value] + [flip(value, "hid", stride * k) for k in range(1, members)])
    return value


def gather_pieces(value):
    pieces = {0: value}
    plan = stages(lax.axis_size("hid"))
    for stride, members in plan[1:] + plan[:1]:
        for offset in list(pieces):
            for k in range(1, members):
                pieces[offset ^ (stride * k)] = flip(pieces[offset], "hid", stride * k)
    return list(pieces), list(pieces.values())


def body(section_inputs, w_in, w_out, warm_factor, pending_left, pending_right, incoming_left, incoming_right):
    w_in, w_out, inputs = w_in[0], w_out[0], section_inputs[0]
    ticks, rows_own, depth = inputs.shape
    hidden_units = w_out.shape[0]
    rank = warm_factor.shape[2]
    count, own = lax.axis_size("hid"), lax.axis_index("hid")
    rows = rows_own * count
    sections = lax.axis_size("pipe")
    is_top = lax.axis_index("pipe") == sections - 1
    full = 2 * rows * depth * hidden_units
    turned = lambda value: jnp.swapaxes(value, -1, -2)
    incoming = (turned(incoming_left), turned(incoming_right))
    warm = turned(warm_factor[0])
    places = jnp.stack([own, is_top.astype(own.dtype)]).astype(jnp.int32)
    wide = ((rows, hidden_units), BF16)
    left_form, right_form = ((rank, rows), F32), ((rank, depth), F32)
    chips = count // 2
    direct = stages(count) == [(1, 2), (2, chips)]

    if rows_own % 16 == 0:
        offsets, pieces = gather_pieces(inputs[0])
        _, later = gather_pieces(inputs[1:])
    else:
        gathered = lax.all_gather(inputs, "hid", axis=1, tiled=True)
        offsets, pieces, later = [0], [gathered[0]], [gathered[1:]]
    up, left, right = on_device(
        up_kernel,
        [wide, left_form, right_form],
        (places, *incoming, turned(pending_left[0]), turned(pending_right[0]), w_out),
        full,
        "up",
        1,
    )

    for tick in range(ticks):
        last = tick + 1 == ticks
        warm_in = on_device(
            warm_kernel, ((2 * rank, hidden_units), BF16), (warm, w_in), full // 2, "warm"
        )
        scratch = [pltpu.VMEM((rows, depth), BF16)]
        if tick == 0:
            hidden, proj = on_device(
                functools.partial(first_kernel, offsets),
                [wide, left_form],
                (places, *pieces, w_in, up, warm_in, left, right, warm),
                full,
                "first",
                1,
                scratch,
            )
        else:
            mask = on_device(
                functools.partial(mask_kernel, offsets, tick - 1),
                wide,
                (places, *later, w_in),
                full,
                "mask",
                1,
                scratch,
            )
            hidden, proj, left, right = on_device(
                functools.partial(hidden_kernel, tick),
                [wide, left_form, left_form, right_form],
                (places, *incoming, both, warm, w_out, mask, warm_in),
                full,
                "hidden",
                1,
            )
        merged = on_device(
            merged_kernel, ((rows, depth), F32), (places, left, right, hidden, w_in), full, "merged", 1
        )
        if last and direct:
            outgoing = on_device(
                outgoing_kernel, ((chips, rows_own, depth), BF16), (places, merged), full // 16, "outgoing", 1
            )
            arrived = flip(outgoing, "hid", 1)
        proj = all_sum(proj)
        partial_right = on_device(
            right_kernel, right_form, (proj, merged), full // 16, "right"
        )
        left_new, inverse = on_device(
            factor_kernel, [left_form, ((rank, rank), F32)], (proj,), full // 2, "factor"
        )
        if last and direct:
            packed = ((rows_own + 2 * rank, depth), BF16)
            own_rows, own_right, *packs = on_device(
                functools.partial(pack_kernel, chips),
                [((rows_own, depth), F32), right_form] + [packed] * (chips - 1),
                (places, merged, arrived, partial_right, flip(partial_right, "hid", 1)),
                full // 16,
                "pack",
                1,
            )
            packs = [flip(pack, "hid", 2 * k) for k, pack in enumerate(packs, 1)]
            grads, warm = on_device(
                last_kernel,
                [((rows_own, depth), F32), right_form],
                (inverse, own_rows, own_right, *packs),
                full // 16,
                "last",
            )
            break
        if last:
            grads = lax.psum_scatter(merged, "hid", scatter_dimension=0, tiled=True)
        warm, both = on_device(
            finish_kernel,
            [right_form, ((rank, rows + depth), F32)],
            (inverse, left_new, all_sum(partial_right)),
            full // 16,
            "finish",
        )
        if not last:
            both = lax.ppermute(both, "pipe", [(source, source - 1) for source in range(1, sections)])
    left_rows = lax.dynamic_slice_in_dim(left_new, own * rows_own, rows_own, 1)
    return grads[None], turned(left_rows)[None], turned(warm)[None]


def solution(mesh):
    placed = (
        P("pipe", None, "hid", None),
        P("pipe", None, "hid"),
        P("pipe", "hid", None),
        P("pipe", None, None),
        P("pipe", None, None),
        P("pipe", None, None),
        P(),
        P(),
    )
    return jax.shard_map(
        body,
        mesh=mesh,
        in_specs=placed,
        out_specs=(P("pipe", "hid", None), P("pipe", "hid", None), P("pipe", None, None)),
        check_vma=False,
    )
```

```python
import functools

import jax
import jax.numpy as jnp
from jax import lax
from jax.experimental import pallas as pl
from jax.experimental.pallas import tpu as pltpu
from jax.sharding import PartitionSpec as P

F32 = jnp.float32
BF16 = jnp.bfloat16
HIGH = lax.Precision.HIGHEST
VMEM = pl.BlockSpec(memory_space=pltpu.VMEM)
HBM = pl.BlockSpec(memory_space=pltpu.HBM)
MIB = 1 << 20


def dot(first, second, first_dim, second_dim, precision=None):
    return lax.dot_general(
        first,
        second,
        (((first_dim,), (second_dim,)), ((), ())),
        precision=precision,
        preferred_element_type=F32,
    )


def split(value):
    high = value.astype(BF16)
    low = (value - high.astype(F32)).astype(BF16)
    return jnp.concatenate([high, low], 0)


def chunks(total, most=512):
    size = min(total, most)
    return [(start, size) for start in range(0, total, size)]


def left_parts(left_t):
    left = left_t.T
    high = left.astype(BF16)
    low = (left - high.astype(F32)).astype(BF16)
    return jnp.concatenate([high, high, low], 1)


def right_parts(right_t):
    high = right_t.astype(BF16)
    low = (right_t - high.astype(F32)).astype(BF16)
    return jnp.concatenate([high, low, high], 0)


def cotangent_of(lefts, right_t):
    return dot(lefts, right_parts(right_t), 1, 0)


def chosen(incoming, other):
    return jnp.where(lax.axis_index("pipe") == lax.axis_size("pipe") - 1, incoming, other)


def own_columns(depth):
    share = depth // lax.axis_size("hid")
    if share % 128 == 0:
        return pl.ds(pl.multiple_of(lax.axis_index("hid") * share, share), share), 1.0
    return slice(0, depth), jnp.where(lax.axis_index("hid") == 0, 1.0, 0.0)


def own_width(depth):
    share = depth // lax.axis_size("hid")
    return share if share % 128 == 0 else depth


def on_device(kernel, outs, operands, flops, name, scratch=(), far=0, limit=8):
    many = isinstance(outs, list)
    shapes = [jax.ShapeDtypeStruct(*out) for out in (outs if many else [outs])]
    result = pl.pallas_call(
        kernel,
        out_shape=shapes,
        in_specs=[VMEM] * (len(operands) - far) + [HBM] * far,
        out_specs=[VMEM] * len(shapes),
        scratch_shapes=list(scratch),
        compiler_params=pltpu.CompilerParams(vmem_limit_bytes=limit * MIB),
        cost_estimate=pl.CostEstimate(flops=flops, bytes_accessed=1 << 20, transcendentals=0),
        name=name,
    )(*operands)
    return result if many else result[0]


def fetch(pairs, sems):
    copies = [pltpu.make_async_copy(source, target, sems.at[k]) for k, (source, target) in enumerate(pairs)]
    for copy in copies:
        copy.start()
    return copies


def up_kernel(
    in_left, in_right, pend_left, pend_right, warm_ref, w_out,
    up_ref, block_ref, proj_ref, w_out_ref, right_ref, sems,
):
    parts = chunks(w_out_ref.shape[0], 1024)
    arrivals = fetch([(w_out.at[pl.ds(*part)], w_out_ref.at[pl.ds(*part)]) for part in parts], sems)
    left = chosen(in_left[0], pend_left[...])
    right_ref[...] = chosen(in_right[0], pend_right[...])
    lefts = left_parts(left)
    own_share(lefts, right_ref, warm_ref, block_ref, proj_ref)
    cotangent_low = cotangent_of(lefts, right_ref[...]).astype(BF16)
    for part, (start, size) in enumerate(parts):
        arrivals[part].wait()
        up_ref[:, start : start + size] = dot(cotangent_low, w_out_ref[start : start + size, :], 1, 1).astype(BF16)


def own_share(lefts, right_ref, warm_ref, block_ref, proj_ref):
    here, factor = own_columns(right_ref.shape[1])
    block = cotangent_of(lefts, right_ref[:, here]) * factor
    block_ref[...] = block
    high = block.astype(BF16)
    low = (block - high.astype(F32)).astype(BF16)
    warm = split(warm_ref[:, here])
    proj_ref[...] = jnp.zeros_like(proj_ref)
    add_projected(dot(high, warm, 1, 1) + dot(low, warm, 1, 1), proj_ref)


def warm_into(stacked, w_in_ref, out_ref, start, size):
    rank = stacked.shape[0] // 2
    both = dot(stacked, w_in_ref[:, start : start + size], 1, 0)
    out_ref[:, start : start + size] = split(both[:rank] + both[rank:])


def warm_kernel(warm_ref, w_in_ref, out_ref):
    stacked = split(warm_ref[...])
    for start, size in chunks(w_in_ref.shape[1]):
        warm_into(stacked, w_in_ref, out_ref, start, size)


def enter_kernel(warm_ref, w_in, out_ref, w_in_ref, sems):
    parts = chunks(w_in_ref.shape[1])
    arrivals = fetch([(w_in.at[:, pl.ds(*part)], w_in_ref.at[:, pl.ds(*part)]) for part in parts], sems)
    stacked = split(warm_ref[...])
    for part, (start, size) in enumerate(parts):
        arrivals[part].wait()
        warm_into(stacked, w_in_ref, out_ref, start, size)


def place_rows(offsets, pieces, rows_ref):
    block = pieces[0].shape[0]
    for offset, piece in zip(offsets, pieces):
        place = 0
        if len(pieces) > 1:
            place = pl.multiple_of(jnp.bitwise_xor(lax.axis_index("hid"), offset) * block, block)
        rows_ref[pl.ds(place, block), :] = piece[...]


def project(hidden, warm_in_ref, start, size, total):
    part = dot(hidden, warm_in_ref[:, start : start + size], 1, 1)
    return part if total is None else total + part


def add_projected(total, proj_ref):
    rank = proj_ref.shape[0]
    turned = total.T
    proj_ref[...] += turned[:rank] + turned[rank:]


def first_kernel(offsets, *refs):
    pieces, rest = refs[: len(offsets)], refs[len(offsets) :]
    w_in_ref, up_ref, warm_in_ref, share_ref, hidden_ref, proj_ref, rows_ref = rest
    place_rows(offsets, [piece.at[0] for piece in pieces], rows_ref)
    total = None
    for start, size in chunks(w_in_ref.shape[1]):
        preact = dot(rows_ref[...], w_in_ref[:, start : start + size], 1, 0)
        hidden = jnp.where(preact > 0, up_ref[:, start : start + size].astype(F32), 0.0).astype(BF16)
        hidden_ref[:, start : start + size] = hidden
        total = project(hidden, warm_in_ref, start, size, total)
    proj_ref[...] = share_ref[...]
    add_projected(total, proj_ref)


def mask_kernel(offsets, step, *refs):
    pieces, (w_in_ref, _, mask_ref, rows_ref) = refs[: len(offsets)], refs[len(offsets) :]
    place_rows(offsets, [piece.at[step] for piece in pieces], rows_ref)
    for start, size in chunks(w_in_ref.shape[1]):
        preact = dot(rows_ref[...], w_in_ref[:, start : start + size], 1, 0)
        mask_ref[:, start : start + size] = jnp.where(preact > 0, 1.0, 0.0).astype(BF16)


def hidden_kernel(
    tick, in_left_ref, in_right_ref, both_ref, warm_ref, w_out_ref, mask_ref, warm_in_ref,
    hidden_ref, proj_ref, block_ref, right_ref,
):
    rows = hidden_ref.shape[0]
    lefts = left_parts(chosen(in_left_ref[tick], both_ref[:, :rows]))
    right_ref[...] = chosen(in_right_ref[tick], both_ref[:, rows:])
    cotangent_low = cotangent_of(lefts, right_ref[...]).astype(BF16)
    own_share(lefts, right_ref, warm_ref, block_ref, proj_ref)
    total = None
    for start, size in chunks(w_out_ref.shape[0]):
        up = dot(cotangent_low, w_out_ref[start : start + size, :], 1, 1)
        mask = mask_ref[:, start : start + size]
        hidden = jnp.where(mask.astype(F32) > 0, up, 0.0).astype(BF16)
        hidden_ref[:, start : start + size] = hidden
        total = project(hidden, warm_in_ref, start, size, total)
    add_projected(total, proj_ref)


def merged_kernel(block_ref, hidden_ref, w_in_ref, merged_ref):
    depth = w_in_ref.shape[0]
    size = min(depth, 256)
    for start in range(0, depth, size):
        here = slice(start, start + size)
        merged_ref[:, here] = dot(hidden_ref[...], w_in_ref[here, :], 1, 1)
    here, _ = own_columns(depth)
    merged_ref[:, here] += block_ref[...]


def right_kernel(proj_ref, merged_ref, out_ref):
    stacked = split(proj_ref[...])
    rank = proj_ref.shape[0]
    merged = merged_ref[...]
    high = merged.astype(BF16)
    low = (merged - high.astype(F32)).astype(BF16)
    both = dot(stacked, high, 1, 0) + dot(stacked, low, 1, 0)
    out_ref[...] = both[:rank] + both[rank:]


def factor_kernel(proj_ref, left_ref, inverse_ref):
    proj = proj_ref[...]
    rank = proj.shape[0]
    gram = dot(proj, proj, 1, 1, HIGH)
    line = lax.broadcasted_iota(jnp.int32, (rank, rank), 0)
    column = lax.broadcasted_iota(jnp.int32, (rank, rank), 1)
    eye = jnp.where(line == column, 1.0, 0.0)
    inverse = eye
    for step in range(rank):
        pivot_row = gram[step : step + 1, :]
        pivot = gram[step : step + 1, step : step + 1]
        scale = jnp.where(line[:, :1] > step, gram[:, step : step + 1] / pivot, 0.0)
        inverse = inverse - scale * inverse[step : step + 1, :]
        gram = gram - scale * pivot_row
    pivots = jnp.sum(gram * eye, axis=1, keepdims=True)
    inverse = inverse * lax.rsqrt(pivots)
    inverse_ref[...] = inverse
    left_ref[...] = dot(inverse, proj, 1, 0, HIGH)


def finish_kernel(inverse_ref, left_ref, sums_ref, right_ref, both_ref):
    right = dot(inverse_ref[...], sums_ref[...], 1, 0, HIGH)
    rows = left_ref.shape[1]
    right_ref[...] = right
    both_ref[:, :rows] = left_ref[...]
    both_ref[:, rows:] = right


def outgoing_kernel(merged_ref, out_ref):
    block = out_ref.shape[1]
    for chip in range(out_ref.shape[0]):
        start = pl.multiple_of((2 * chip + 1 - lax.axis_index("hid") % 2) * block, block)
        out_ref[chip] = merged_ref[pl.ds(start, block), :].astype(BF16)


def pack_kernel(chips, merged_ref, arrived_ref, right_ref, right_arrived_ref, own_ref, right_out, *out_refs):
    block = own_ref.shape[0]
    core, chip = lax.axis_index("hid") % 2, lax.axis_index("hid") // 2
    stacked = split(right_ref[...] + right_arrived_ref[...])
    rank = right_ref.shape[0]
    right_out[...] = stacked[:rank].astype(F32) + stacked[rank:].astype(F32)
    for turn in range(chips):
        target = jnp.bitwise_xor(chip, turn)
        start = pl.multiple_of((2 * target + core) * block, block)
        value = merged_ref[pl.ds(start, block), :] + arrived_ref[target].astype(F32)
        if turn:
            out_refs[turn - 1][:block, :] = value.astype(BF16)
            out_refs[turn - 1][block:, :] = stacked
        else:
            own_ref[...] = value


def last_kernel(inverse_ref, own_ref, right_own_ref, *refs):
    packs, (grads_ref, right_ref) = refs[:-2], refs[-2:]
    block, rank = own_ref.shape[0], inverse_ref.shape[0]
    rows = [own_ref[...]] + [pack[:block, :].astype(F32) for pack in packs]
    sums = [right_own_ref[...]] + [
        pack[block : block + rank, :].astype(F32) + pack[block + rank :, :].astype(F32) for pack in packs
    ]
    grads_ref[...] = tree_sum(rows)
    right_ref[...] = dot(inverse_ref[...], tree_sum(sums), 1, 0, HIGH)


def flip(value, axis, bits):
    count = lax.axis_size(axis)
    return lax.ppermute(value, axis, [(source, source ^ bits) for source in range(count)])


def stages(count):
    found, stride = [], 1
    while stride < count:
        members = 2 if stride == 1 else min(4, count // stride)
        found.append((stride, members))
        stride *= members
    return found


def tree_sum(parts):
    while len(parts) > 1:
        parts = [first + second for first, second in zip(parts[::2], parts[1::2])]
    return parts[0]


def all_sum(value):
    for stride, members in stages(lax.axis_size("hid")):
        value = tree_sum([value] + [flip(value, "hid", stride * k) for k in range(1, members)])
    return value


def gather_pieces(pieces, plan):
    pieces = dict(pieces)
    for stride, members in plan:
        for offset in list(pieces):
            for k in range(1, members):
                pieces[offset ^ (stride * k)] = flip(pieces[offset], "hid", stride * k)
    return pieces


def body(section_inputs, w_in, w_out, warm_factor, pending_left, pending_right, incoming_left, incoming_right):
    w_in, w_out, inputs = w_in[0], w_out[0], section_inputs[0]
    ticks, rows_own, depth = inputs.shape
    hidden_units = w_out.shape[0]
    rank = warm_factor.shape[2]
    count, own = lax.axis_size("hid"), lax.axis_index("hid")
    rows = rows_own * count
    sections = lax.axis_size("pipe")
    full = 2 * rows * depth * hidden_units
    turned = lambda value: jnp.swapaxes(value, -1, -2)
    incoming = (turned(incoming_left), turned(incoming_right))
    warm = turned(warm_factor[0])
    wide = ((rows, hidden_units), BF16)
    left_form, right_form = ((rank, rows), F32), ((rank, depth), F32)
    chips = count // 2
    direct = stages(count) == [(1, 2), (2, chips)]

    plan = stages(count)
    by_rows = rows_own % 16 == 0
    if by_rows:
        blocks = gather_pieces({0: inputs}, plan[1:])
    else:
        blocks = {0: lax.all_gather(inputs, "hid", axis=1, tiled=True)}
    block_form = ((rows, own_width(depth)), F32)
    sems = [pltpu.SemaphoreType.DMA((len(chunks(hidden_units)),))]
    warm_in, w_in = on_device(
        enter_kernel,
        [((2 * rank, hidden_units), BF16), (w_in.shape, BF16)],
        (warm, w_in),
        full,
        "enter",
        sems,
        1,
        43,
    )
    early = lax.optimization_barrier((warm, warm_in))[0]
    up, block, share, w_out = on_device(
        up_kernel,
        [wide, block_form, left_form, (w_out.shape, BF16)],
        (*incoming, turned(pending_left[0]), turned(pending_right[0]), early, w_out),
        full,
        "up",
        [pltpu.VMEM(*right_form)] + sems,
        1,
        38,
    )
    if by_rows:
        held = lax.optimization_barrier((list(blocks.values()), share))[0]
        blocks = gather_pieces(zip(blocks, held), plan[:1])
    offsets, pieces = list(blocks), list(blocks.values())

    for tick in range(ticks):
        last = tick + 1 == ticks
        scratch = [pltpu.VMEM((rows, depth), BF16)]
        if tick == 0:
            hidden, proj = on_device(
                functools.partial(first_kernel, offsets),
                [wide, left_form],
                (*pieces, w_in, up, warm_in, share),
                full,
                "first",
                scratch,
            )
        else:
            warm_in = on_device(
                warm_kernel, ((2 * rank, hidden_units), BF16), (warm, w_in), full // 2, "warm"
            )
            mask = on_device(
                functools.partial(mask_kernel, offsets, tick),
                wide,
                (*pieces, w_in, leaving),
                full,
                "mask",
                scratch,
            )
            hidden, proj, block = on_device(
                functools.partial(hidden_kernel, tick),
                [wide, left_form, block_form],
                (*incoming, both, warm, w_out, mask, warm_in),
                full,
                "hidden",
                [pltpu.VMEM(*right_form)],
            )
        merged = on_device(merged_kernel, ((rows, depth), F32), (block, hidden, w_in), full, "merged")
        if last and direct:
            outgoing = on_device(
                outgoing_kernel, ((chips, rows_own, depth), BF16), (merged,), full // 16, "outgoing"
            )
            arrived = flip(outgoing, "hid", 1)
        proj = all_sum(proj)
        partial_right = on_device(
            right_kernel, right_form, (proj, merged), full // 16, "right"
        )
        left_new, inverse = on_device(
            factor_kernel, [left_form, ((rank, rank), F32)], (proj,), full // 2, "factor"
        )
        if last and direct:
            packed = ((rows_own + 2 * rank, depth), BF16)
            own_rows, own_right, *packs = on_device(
                functools.partial(pack_kernel, chips),
                [((rows_own, depth), F32), right_form] + [packed] * (chips - 1),
                (merged, arrived, partial_right, flip(partial_right, "hid", 1)),
                full // 16,
                "pack",
            )
            packs = [flip(pack, "hid", 2 * k) for k, pack in enumerate(packs, 1)]
            grads, warm = on_device(
                last_kernel,
                [((rows_own, depth), F32), right_form],
                (inverse, own_rows, own_right, *packs),
                full // 16,
                "last",
            )
            break
        if last:
            grads = lax.psum_scatter(merged, "hid", scatter_dimension=0, tiled=True)
        warm, leaving = on_device(
            finish_kernel,
            [right_form, ((rank, rows + depth), F32)],
            (inverse, left_new, all_sum(partial_right)),
            full // 16,
            "finish",
        )
        if not last:
            both = lax.ppermute(leaving, "pipe", [(source, source - 1) for source in range(1, sections)])
    left_rows = lax.dynamic_slice_in_dim(left_new, own * rows_own, rows_own, 1)
    return grads[None], turned(left_rows)[None], turned(warm)[None]


def solution(mesh):
    placed = (
        P("pipe", None, "hid", None),
        P("pipe", None, "hid"),
        P("pipe", "hid", None),
        P("pipe", None, None),
        P("pipe", None, None),
        P("pipe", None, None),
        P(),
        P(),
    )
    return jax.shard_map(
        body,
        mesh=mesh,
        in_specs=placed,
        out_specs=(P("pipe", "hid", None), P("pipe", "hid", None), P("pipe", None, None)),
        check_vma=False,
    )
```

```python
import functools

import jax
import jax.numpy as jnp
from jax import lax
from jax.experimental import pallas as pl
from jax.experimental.pallas import tpu as pltpu
from jax.sharding import PartitionSpec as P

F32 = jnp.float32
BF16 = jnp.bfloat16
HIGH = lax.Precision.HIGHEST
VMEM = pl.BlockSpec(memory_space=pltpu.VMEM)
HBM = pl.BlockSpec(memory_space=pltpu.HBM)
MIB = 1 << 20


def dot(first, second, first_dim, second_dim, precision=None):
    return lax.dot_general(
        first,
        second,
        (((first_dim,), (second_dim,)), ((), ())),
        precision=precision,
        preferred_element_type=F32,
    )


def split(value):
    high = value.astype(BF16)
    low = (value - high.astype(F32)).astype(BF16)
    return jnp.concatenate([high, low], 0)


def chunks(total, most=512):
    size = min(total, most)
    return [(start, size) for start in range(0, total, size)]


def left_parts(left_t):
    left = left_t.T
    high = left.astype(BF16)
    low = (left - high.astype(F32)).astype(BF16)
    return jnp.concatenate([high, high, low], 1)


def right_parts(right_t):
    high = right_t.astype(BF16)
    low = (right_t - high.astype(F32)).astype(BF16)
    return jnp.concatenate([high, low, high], 0)


def cotangent_of(lefts, right_t):
    return dot(lefts, right_parts(right_t), 1, 0)


def chosen(incoming, other):
    return jnp.where(lax.axis_index("pipe") == lax.axis_size("pipe") - 1, incoming, other)


def own_columns(depth):
    share = depth // lax.axis_size("hid")
    if share % 128 == 0:
        return pl.ds(pl.multiple_of(lax.axis_index("hid") * share, share), share), 1.0
    return slice(0, depth), jnp.where(lax.axis_index("hid") == 0, 1.0, 0.0)


def own_width(depth):
    share = depth // lax.axis_size("hid")
    return share if share % 128 == 0 else depth


def on_device(kernel, outs, operands, flops, name, scratch=(), far=0, limit=8):
    many = isinstance(outs, list)
    shapes = [jax.ShapeDtypeStruct(*out) for out in (outs if many else [outs])]
    result = pl.pallas_call(
        kernel,
        out_shape=shapes,
        in_specs=[VMEM] * (len(operands) - far) + [HBM] * far,
        out_specs=[VMEM] * len(shapes),
        scratch_shapes=list(scratch),
        compiler_params=pltpu.CompilerParams(vmem_limit_bytes=limit * MIB),
        cost_estimate=pl.CostEstimate(flops=flops, bytes_accessed=1 << 20, transcendentals=0),
        name=name,
    )(*operands)
    return result if many else result[0]


def begin_kernel(rows_ref, first_ref, later_ref):
    first_ref[...] = rows_ref[0]
    later_ref[...] = rows_ref[1:]


def up_kernel(in_left, in_right, pend_left, pend_right, warm_ref, w_out_ref, up_ref, block_ref, proj_ref, right_ref):
    left = chosen(in_left[0], pend_left[...])
    right_ref[...] = chosen(in_right[0], pend_right[...])
    lefts = left_parts(left)
    own_share(lefts, right_ref, warm_ref, block_ref, proj_ref)
    cotangent_low = cotangent_of(lefts, right_ref[...]).astype(BF16)
    for start, size in chunks(w_out_ref.shape[0]):
        up_ref[:, start : start + size] = dot(cotangent_low, w_out_ref[start : start + size, :], 1, 1).astype(BF16)


def own_share(lefts, right_ref, warm_ref, block_ref, proj_ref):
    here, factor = own_columns(right_ref.shape[1])
    block = cotangent_of(lefts, right_ref[:, here]) * factor
    block_ref[...] = block
    high = block.astype(BF16)
    low = (block - high.astype(F32)).astype(BF16)
    warm = split(warm_ref[:, here])
    proj_ref[...] = jnp.zeros_like(proj_ref)
    add_projected(dot(high, warm, 1, 1) + dot(low, warm, 1, 1), proj_ref)


def warm_into(stacked, w_in_ref, out_ref, start, size):
    rank = stacked.shape[0] // 2
    both = dot(stacked, w_in_ref[:, start : start + size], 1, 0)
    out_ref[:, start : start + size] = split(both[:rank] + both[rank:])


def warm_kernel(warm_ref, w_in_ref, out_ref):
    stacked = split(warm_ref[...])
    for start, size in chunks(w_in_ref.shape[1]):
        warm_into(stacked, w_in_ref, out_ref, start, size)


def place_rows(offsets, pieces, rows_ref):
    block = pieces[0].shape[0]
    for offset, piece in zip(offsets, pieces):
        place = 0
        if len(pieces) > 1:
            place = pl.multiple_of(jnp.bitwise_xor(lax.axis_index("hid"), offset) * block, block)
        rows_ref[pl.ds(place, block), :] = piece[...]


def project(hidden, warm_in_ref, start, size, total):
    part = dot(hidden, warm_in_ref[:, start : start + size], 1, 1)
    return part if total is None else total + part


def add_projected(total, proj_ref):
    rank = proj_ref.shape[0]
    turned = total.T
    proj_ref[...] += turned[:rank] + turned[rank:]


def first_kernel(offsets, *refs):
    pieces, rest = refs[: len(offsets)], refs[len(offsets) :]
    w_in_ref, up_ref, warm_in_ref, share_ref, hidden_ref, proj_ref, rows_ref = rest
    place_rows(offsets, pieces, rows_ref)
    total = None
    for start, size in chunks(w_in_ref.shape[1]):
        preact = dot(rows_ref[...], w_in_ref[:, start : start + size], 1, 0)
        hidden = jnp.where(preact > 0, up_ref[:, start : start + size].astype(F32), 0.0).astype(BF16)
        hidden_ref[:, start : start + size] = hidden
        total = project(hidden, warm_in_ref, start, size, total)
    proj_ref[...] = share_ref[...]
    add_projected(total, proj_ref)


def mask_kernel(offsets, step, *refs):
    pieces, (w_in_ref, _, mask_ref, rows_ref) = refs[: len(offsets)], refs[len(offsets) :]
    place_rows(offsets, [piece.at[step] for piece in pieces], rows_ref)
    for start, size in chunks(w_in_ref.shape[1]):
        preact = dot(rows_ref[...], w_in_ref[:, start : start + size], 1, 0)
        mask_ref[:, start : start + size] = jnp.where(preact > 0, 1.0, 0.0).astype(BF16)


def hidden_kernel(
    tick, in_left_ref, in_right_ref, both_ref, warm_ref, w_out_ref, mask_ref, warm_in_ref,
    hidden_ref, proj_ref, block_ref, right_ref,
):
    rows = hidden_ref.shape[0]
    lefts = left_parts(chosen(in_left_ref[tick], both_ref[:, :rows]))
    right_ref[...] = chosen(in_right_ref[tick], both_ref[:, rows:])
    cotangent_low = cotangent_of(lefts, right_ref[...]).astype(BF16)
    own_share(lefts, right_ref, warm_ref, block_ref, proj_ref)
    total = None
    for start, size in chunks(w_out_ref.shape[0]):
        up = dot(cotangent_low, w_out_ref[start : start + size, :], 1, 1)
        mask = mask_ref[:, start : start + size]
        hidden = jnp.where(mask.astype(F32) > 0, up, 0.0).astype(BF16)
        hidden_ref[:, start : start + size] = hidden
        total = project(hidden, warm_in_ref, start, size, total)
    add_projected(total, proj_ref)


def merged_kernel(block_ref, hidden_ref, w_in_ref, merged_ref):
    depth = w_in_ref.shape[0]
    size = min(depth, 256)
    for start in range(0, depth, size):
        here = slice(start, start + size)
        merged_ref[:, here] = dot(hidden_ref[...], w_in_ref[here, :], 1, 1)
    here, _ = own_columns(depth)
    merged_ref[:, here] += block_ref[...]


def right_kernel(proj_ref, merged_ref, out_ref):
    stacked = split(proj_ref[...])
    rank = proj_ref.shape[0]
    merged = merged_ref[...]
    high = merged.astype(BF16)
    low = (merged - high.astype(F32)).astype(BF16)
    both = dot(stacked, high, 1, 0) + dot(stacked, low, 1, 0)
    out_ref[...] = both[:rank] + both[rank:]


def factor_kernel(proj_ref, left_ref, inverse_ref):
    proj = proj_ref[...]
    rank = proj.shape[0]
    gram = dot(proj, proj, 1, 1, HIGH)
    line = lax.broadcasted_iota(jnp.int32, (rank, rank), 0)
    column = lax.broadcasted_iota(jnp.int32, (rank, rank), 1)
    eye = jnp.where(line == column, 1.0, 0.0)
    inverse = eye
    for step in range(rank):
        pivot_row = gram[step : step + 1, :]
        pivot = gram[step : step + 1, step : step + 1]
        scale = jnp.where(line[:, :1] > step, gram[:, step : step + 1] / pivot, 0.0)
        inverse = inverse - scale * inverse[step : step + 1, :]
        gram = gram - scale * pivot_row
    pivots = jnp.sum(gram * eye, axis=1, keepdims=True)
    inverse = inverse * lax.rsqrt(pivots)
    inverse_ref[...] = inverse
    left_ref[...] = dot(inverse, proj, 1, 0, HIGH)


def finish_kernel(inverse_ref, left_ref, sums_ref, right_ref, both_ref):
    right = dot(inverse_ref[...], sums_ref[...], 1, 0, HIGH)
    rows = left_ref.shape[1]
    right_ref[...] = right
    both_ref[:, :rows] = left_ref[...]
    both_ref[:, rows:] = right


def outgoing_kernel(merged_ref, out_ref):
    block = out_ref.shape[1]
    for chip in range(out_ref.shape[0]):
        start = pl.multiple_of((2 * chip + 1 - lax.axis_index("hid") % 2) * block, block)
        out_ref[chip] = merged_ref[pl.ds(start, block), :].astype(BF16)


def pack_kernel(chips, merged_ref, arrived_ref, right_ref, right_arrived_ref, own_ref, right_out, *out_refs):
    block = own_ref.shape[0]
    core, chip = lax.axis_index("hid") % 2, lax.axis_index("hid") // 2
    stacked = split(right_ref[...] + right_arrived_ref[...])
    rank = right_ref.shape[0]
    right_out[...] = stacked[:rank].astype(F32) + stacked[rank:].astype(F32)
    for turn in range(chips):
        target = jnp.bitwise_xor(chip, turn)
        start = pl.multiple_of((2 * target + core) * block, block)
        value = merged_ref[pl.ds(start, block), :] + arrived_ref[target].astype(F32)
        if turn:
            out_refs[turn - 1][:block, :] = value.astype(BF16)
            out_refs[turn - 1][block:, :] = stacked
        else:
            own_ref[...] = value


def last_kernel(inverse_ref, own_ref, right_own_ref, *refs):
    packs, (grads_ref, right_ref) = refs[:-2], refs[-2:]
    block, rank = own_ref.shape[0], inverse_ref.shape[0]
    rows = [own_ref[...]] + [pack[:block, :].astype(F32) for pack in packs]
    sums = [right_own_ref[...]] + [
        pack[block : block + rank, :].astype(F32) + pack[block + rank :, :].astype(F32) for pack in packs
    ]
    grads_ref[...] = tree_sum(rows)
    right_ref[...] = dot(inverse_ref[...], tree_sum(sums), 1, 0, HIGH)


def flip(value, axis, bits):
    count = lax.axis_size(axis)
    return lax.ppermute(value, axis, [(source, source ^ bits) for source in range(count)])


def stages(count):
    found, stride = [], 1
    while stride < count:
        members = 2 if stride == 1 else min(4, count // stride)
        found.append((stride, members))
        stride *= members
    return found


def tree_sum(parts):
    while len(parts) > 1:
        parts = [first + second for first, second in zip(parts[::2], parts[1::2])]
    return parts[0]


def all_sum(value):
    for stride, members in stages(lax.axis_size("hid")):
        value = tree_sum([value] + [flip(value, "hid", stride * k) for k in range(1, members)])
    return value


def gather_pieces(pieces, plan):
    pieces = dict(pieces)
    for stride, members in plan:
        for offset in list(pieces):
            for k in range(1, members):
                pieces[offset ^ (stride * k)] = flip(pieces[offset], "hid", stride * k)
    return pieces


def body(section_inputs, w_in, w_out, warm_factor, pending_left, pending_right, incoming_left, incoming_right):
    w_in, w_out, inputs = w_in[0], w_out[0], section_inputs[0]
    ticks, rows_own, depth = inputs.shape
    hidden_units = w_out.shape[0]
    rank = warm_factor.shape[2]
    count, own = lax.axis_size("hid"), lax.axis_index("hid")
    rows = rows_own * count
    sections = lax.axis_size("pipe")
    full = 2 * rows * depth * hidden_units
    turned = lambda value: jnp.swapaxes(value, -1, -2)
    incoming = (turned(incoming_left), turned(incoming_right))
    warm = turned(warm_factor[0])
    wide = ((rows, hidden_units), BF16)
    left_form, right_form = ((rank, rows), F32), ((rank, depth), F32)
    chips = count // 2
    direct = stages(count) == [(1, 2), (2, chips)]

    plan = stages(count)
    by_rows = rows_own % 16 == 0
    if by_rows:
        rows_first, rows_later = on_device(
            begin_kernel,
            [(inputs.shape[1:], BF16), ((ticks - 1, rows_own, depth), BF16)],
            (inputs,),
            8 * full,
            "begin",
        )
        blocks = gather_pieces({0: rows_first}, plan[1:] + plan[:1])
        later = gather_pieces({0: rows_later}, plan[1:] + plan[:1])
        offsets, pieces, later = list(blocks), list(blocks.values()), list(later.values())
    else:
        everything = lax.all_gather(inputs, "hid", axis=1, tiled=True)
        offsets, pieces, later = [0], [everything[0]], [everything[1:]]
    block_form = ((rows, own_width(depth)), F32)
    warm_in = on_device(warm_kernel, ((2 * rank, hidden_units), BF16), (warm, w_in), full // 2, "warm")
    up, block, share = on_device(
        up_kernel,
        [wide, block_form, left_form],
        (*incoming, turned(pending_left[0]), turned(pending_right[0]), warm, w_out),
        full,
        "up",
        [pltpu.VMEM(*right_form)],
    )

    for tick in range(ticks):
        last = tick + 1 == ticks
        scratch = [pltpu.VMEM((rows, depth), BF16)]
        if tick == 0:
            hidden, proj = on_device(
                functools.partial(first_kernel, offsets),
                [wide, left_form],
                (*pieces, w_in, up, warm_in, share),
                full,
                "first",
                scratch,
            )
        else:
            warm_in = on_device(
                warm_kernel, ((2 * rank, hidden_units), BF16), (warm, w_in), full // 2, "warm"
            )
            mask = on_device(
                functools.partial(mask_kernel, offsets, tick - 1),
                wide,
                (*later, w_in, leaving),
                full,
                "mask",
                scratch,
            )
            hidden, proj, block = on_device(
                functools.partial(hidden_kernel, tick),
                [wide, left_form, block_form],
                (*incoming, both, warm, w_out, mask, warm_in),
                full,
                "hidden",
                [pltpu.VMEM(*right_form)],
            )
        merged = on_device(merged_kernel, ((rows, depth), F32), (block, hidden, w_in), full, "merged")
        if last and direct:
            outgoing = on_device(
                outgoing_kernel, ((chips, rows_own, depth), BF16), (merged,), full // 16, "outgoing"
            )
            arrived = flip(outgoing, "hid", 1)
        proj = all_sum(proj)
        partial_right = on_device(
            right_kernel, right_form, (proj, merged), full // 16, "right"
        )
        left_new, inverse = on_device(
            factor_kernel, [left_form, ((rank, rank), F32)], (proj,), full // 2, "factor"
        )
        if last and direct:
            packed = ((rows_own + 2 * rank, depth), BF16)
            own_rows, own_right, *packs = on_device(
                functools.partial(pack_kernel, chips),
                [((rows_own, depth), F32), right_form] + [packed] * (chips - 1),
                (merged, arrived, partial_right, flip(partial_right, "hid", 1)),
                full // 16,
                "pack",
            )
            packs = [flip(pack, "hid", 2 * k) for k, pack in enumerate(packs, 1)]
            grads, warm = on_device(
                last_kernel,
                [((rows_own, depth), F32), right_form],
                (inverse, own_rows, own_right, *packs),
                full // 16,
                "last",
            )
            break
        if last:
            grads = lax.psum_scatter(merged, "hid", scatter_dimension=0, tiled=True)
        warm, leaving = on_device(
            finish_kernel,
            [right_form, ((rank, rows + depth), F32)],
            (inverse, left_new, all_sum(partial_right)),
            full // 16,
            "finish",
        )
        if not last:
            both = lax.ppermute(leaving, "pipe", [(source, source - 1) for source in range(1, sections)])
    left_rows = lax.dynamic_slice_in_dim(left_new, own * rows_own, rows_own, 1)
    return grads[None], turned(left_rows)[None], turned(warm)[None]


def solution(mesh):
    placed = (
        P("pipe", None, "hid", None),
        P("pipe", None, "hid"),
        P("pipe", "hid", None),
        P("pipe", None, None),
        P("pipe", None, None),
        P("pipe", None, None),
        P(),
        P(),
    )
    return jax.shard_map(
        body,
        mesh=mesh,
        in_specs=placed,
        out_specs=(P("pipe", "hid", None), P("pipe", "hid", None), P("pipe", None, None)),
        check_vma=False,
    )
```

```python
import functools

import jax
import jax.numpy as jnp
from jax import lax
from jax.experimental import pallas as pl
from jax.experimental.pallas import tpu as pltpu
from jax.sharding import PartitionSpec as P

F32 = jnp.float32
BF16 = jnp.bfloat16
HIGH = lax.Precision.HIGHEST
VMEM = pl.BlockSpec(memory_space=pltpu.VMEM)
HBM = pl.BlockSpec(memory_space=pltpu.HBM)
MIB = 1 << 20


def dot(first, second, first_dim, second_dim, precision=None):
    return lax.dot_general(
        first,
        second,
        (((first_dim,), (second_dim,)), ((), ())),
        precision=precision,
        preferred_element_type=F32,
    )


def split(value):
    high = value.astype(BF16)
    low = (value - high.astype(F32)).astype(BF16)
    return jnp.concatenate([high, low], 0)


def chunks(total, most=512):
    size = min(total, most)
    return [(start, size) for start in range(0, total, size)]


def left_parts(left_t):
    left = left_t.T
    high = left.astype(BF16)
    low = (left - high.astype(F32)).astype(BF16)
    return jnp.concatenate([high, high, low], 1)


def right_parts(right_t):
    high = right_t.astype(BF16)
    low = (right_t - high.astype(F32)).astype(BF16)
    return jnp.concatenate([high, low, high], 0)


def cotangent_of(lefts, right_t):
    return dot(lefts, right_parts(right_t), 1, 0)


def chosen(incoming, other):
    return jnp.where(lax.axis_index("pipe") == lax.axis_size("pipe") - 1, incoming, other)


def own_columns(depth):
    share = depth // lax.axis_size("hid")
    if share % 128 == 0:
        return pl.ds(pl.multiple_of(lax.axis_index("hid") * share, share), share), 1.0
    return slice(0, depth), jnp.where(lax.axis_index("hid") == 0, 1.0, 0.0)


def own_width(depth):
    share = depth // lax.axis_size("hid")
    return share if share % 128 == 0 else depth


def on_device(kernel, outs, operands, flops, name, scratch=(), far=0, limit=8):
    many = isinstance(outs, list)
    shapes = [jax.ShapeDtypeStruct(*out) for out in (outs if many else [outs])]
    result = pl.pallas_call(
        kernel,
        out_shape=shapes,
        in_specs=[VMEM] * (len(operands) - far) + [HBM] * far,
        out_specs=[VMEM] * len(shapes),
        scratch_shapes=list(scratch),
        compiler_params=pltpu.CompilerParams(vmem_limit_bytes=limit * MIB),
        cost_estimate=pl.CostEstimate(flops=flops, bytes_accessed=1 << 20, transcendentals=0),
        name=name,
    )(*operands)
    return result if many else result[0]


def begin_kernel(rows_ref, first_ref, later_ref):
    first_ref[...] = rows_ref[0]
    later_ref[...] = rows_ref[1:]


def up_kernel(in_left, in_right, pend_left, pend_right, warm_ref, w_out_ref, up_ref, block_ref, proj_ref, right_ref):
    left = chosen(in_left[0], pend_left[...])
    right_ref[...] = chosen(in_right[0], pend_right[...])
    lefts = left_parts(left)
    own_share(lefts, right_ref, warm_ref, block_ref, proj_ref)
    cotangent_low = cotangent_of(lefts, right_ref[...]).astype(BF16)
    for start, size in chunks(w_out_ref.shape[0]):
        up_ref[:, start : start + size] = dot(cotangent_low, w_out_ref[start : start + size, :], 1, 1).astype(BF16)


def own_share(lefts, right_ref, warm_ref, block_ref, proj_ref):
    here, factor = own_columns(right_ref.shape[1])
    block = cotangent_of(lefts, right_ref[:, here]) * factor
    block_ref[...] = block
    high = block.astype(BF16)
    low = (block - high.astype(F32)).astype(BF16)
    warm = split(warm_ref[:, here])
    proj_ref[...] = jnp.zeros_like(proj_ref)
    add_projected(dot(high, warm, 1, 1) + dot(low, warm, 1, 1), proj_ref)


def warm_into(stacked, w_in_ref, out_ref, start, size):
    rank = stacked.shape[0] // 2
    both = dot(stacked, w_in_ref[:, start : start + size], 1, 0)
    out_ref[:, start : start + size] = split(both[:rank] + both[rank:])


def warm_kernel(warm_ref, w_in_ref, out_ref):
    stacked = split(warm_ref[...])
    for start, size in chunks(w_in_ref.shape[1]):
        warm_into(stacked, w_in_ref, out_ref, start, size)


def place_rows(offsets, pieces, rows_ref):
    block = pieces[0].shape[0]
    for offset, piece in zip(offsets, pieces):
        place = 0
        if len(pieces) > 1:
            place = pl.multiple_of(jnp.bitwise_xor(lax.axis_index("hid"), offset) * block, block)
        rows_ref[pl.ds(place, block), :] = piece[...]


def project(hidden, warm_in_ref, start, size, total):
    part = dot(hidden, warm_in_ref[:, start : start + size], 1, 1)
    return part if total is None else total + part


def add_projected(total, proj_ref):
    rank = proj_ref.shape[0]
    turned = total.T
    proj_ref[...] += turned[:rank] + turned[rank:]


def first_kernel(offsets, *refs):
    pieces, rest = refs[: len(offsets)], refs[len(offsets) :]
    w_in_ref, up_ref, warm_in_ref, share_ref, hidden_ref, proj_ref, rows_ref = rest
    place_rows(offsets, pieces, rows_ref)
    total = None
    for start, size in chunks(w_in_ref.shape[1]):
        preact = dot(rows_ref[...], w_in_ref[:, start : start + size], 1, 0)
        hidden = jnp.where(preact > 0, up_ref[:, start : start + size].astype(F32), 0.0).astype(BF16)
        hidden_ref[:, start : start + size] = hidden
        total = project(hidden, warm_in_ref, start, size, total)
    proj_ref[...] = share_ref[...]
    add_projected(total, proj_ref)


def mask_kernel(offsets, step, *refs):
    pieces, (w_in_ref, _, mask_ref, rows_ref) = refs[: len(offsets)], refs[len(offsets) :]
    place_rows(offsets, [piece.at[step] for piece in pieces], rows_ref)
    for start, size in chunks(w_in_ref.shape[1]):
        preact = dot(rows_ref[...], w_in_ref[:, start : start + size], 1, 0)
        mask_ref[:, start : start + size] = jnp.where(preact > 0, 1.0, 0.0).astype(BF16)


def hidden_kernel(
    tick, in_left_ref, in_right_ref, both_ref, warm_ref, w_out_ref, mask_ref, warm_in_ref,
    hidden_ref, proj_ref, block_ref, right_ref,
):
    rows = hidden_ref.shape[0]
    lefts = left_parts(chosen(in_left_ref[tick], both_ref[:, :rows]))
    right_ref[...] = chosen(in_right_ref[tick], both_ref[:, rows:])
    cotangent_low = cotangent_of(lefts, right_ref[...]).astype(BF16)
    own_share(lefts, right_ref, warm_ref, block_ref, proj_ref)
    total = None
    for start, size in chunks(w_out_ref.shape[0]):
        up = dot(cotangent_low, w_out_ref[start : start + size, :], 1, 1)
        mask = mask_ref[:, start : start + size]
        hidden = jnp.where(mask.astype(F32) > 0, up, 0.0).astype(BF16)
        hidden_ref[:, start : start + size] = hidden
        total = project(hidden, warm_in_ref, start, size, total)
    add_projected(total, proj_ref)


def merged_kernel(block_ref, hidden_ref, w_in_ref, merged_ref):
    depth = w_in_ref.shape[0]
    size = min(depth, 256)
    for start in range(0, depth, size):
        here = slice(start, start + size)
        merged_ref[:, here] = dot(hidden_ref[...], w_in_ref[here, :], 1, 1)
    here, _ = own_columns(depth)
    merged_ref[:, here] += block_ref[...]


def right_kernel(proj_ref, merged_ref, out_ref):
    stacked = split(proj_ref[...])
    rank = proj_ref.shape[0]
    merged = merged_ref[...]
    high = merged.astype(BF16)
    low = (merged - high.astype(F32)).astype(BF16)
    both = dot(stacked, high, 1, 0) + dot(stacked, low, 1, 0)
    out_ref[...] = both[:rank] + both[rank:]


def factor_kernel(proj_ref, left_ref, inverse_ref):
    proj = proj_ref[...]
    rank = proj.shape[0]
    gram = dot(proj, proj, 1, 1, HIGH)
    line = lax.broadcasted_iota(jnp.int32, (rank, rank), 0)
    column = lax.broadcasted_iota(jnp.int32, (rank, rank), 1)
    eye = jnp.where(line == column, 1.0, 0.0)
    inverse = eye
    for step in range(rank):
        pivot_row = gram[step : step + 1, :]
        pivot = gram[step : step + 1, step : step + 1]
        scale = jnp.where(line[:, :1] > step, gram[:, step : step + 1] / pivot, 0.0)
        inverse = inverse - scale * inverse[step : step + 1, :]
        gram = gram - scale * pivot_row
    pivots = jnp.sum(gram * eye, axis=1, keepdims=True)
    inverse = inverse * lax.rsqrt(pivots)
    inverse_ref[...] = inverse
    left_ref[...] = dot(inverse, proj, 1, 0, HIGH)


def finish_kernel(inverse_ref, left_ref, sums_ref, right_ref, both_ref):
    right = dot(inverse_ref[...], sums_ref[...], 1, 0, HIGH)
    rows = left_ref.shape[1]
    right_ref[...] = right
    both_ref[:, :rows] = left_ref[...]
    both_ref[:, rows:] = right


def outgoing_kernel(merged_ref, out_ref):
    block = out_ref.shape[1]
    for chip in range(out_ref.shape[0]):
        start = pl.multiple_of((2 * chip + 1 - lax.axis_index("hid") % 2) * block, block)
        out_ref[chip] = merged_ref[pl.ds(start, block), :].astype(BF16)


def pack_kernel(chips, merged_ref, arrived_ref, right_ref, right_arrived_ref, own_ref, right_out, *out_refs):
    block = own_ref.shape[0]
    core, chip = lax.axis_index("hid") % 2, lax.axis_index("hid") // 2
    stacked = split(right_ref[...] + right_arrived_ref[...])
    rank = right_ref.shape[0]
    right_out[...] = stacked[:rank].astype(F32) + stacked[rank:].astype(F32)
    for turn in range(chips):
        target = jnp.bitwise_xor(chip, turn)
        start = pl.multiple_of((2 * target + core) * block, block)
        value = merged_ref[pl.ds(start, block), :] + arrived_ref[target].astype(F32)
        if turn:
            out_refs[turn - 1][:block, :] = value.astype(BF16)
            out_refs[turn - 1][block:, :] = stacked
        else:
            own_ref[...] = value


def last_kernel(inverse_ref, own_ref, right_own_ref, *refs):
    packs, (grads_ref, right_ref) = refs[:-2], refs[-2:]
    block, rank = own_ref.shape[0], inverse_ref.shape[0]
    rows = [own_ref[...]] + [pack[:block, :].astype(F32) for pack in packs]
    sums = [right_own_ref[...]] + [
        pack[block : block + rank, :].astype(F32) + pack[block + rank :, :].astype(F32) for pack in packs
    ]
    grads_ref[...] = tree_sum(rows)
    right_ref[...] = dot(inverse_ref[...], tree_sum(sums), 1, 0, HIGH)


def flip(value, axis, bits):
    count = lax.axis_size(axis)
    return lax.ppermute(value, axis, [(source, source ^ bits) for source in range(count)])


def stages(count):
    found, stride = [], 1
    while stride < count:
        members = 2 if stride == 1 else min(4, count // stride)
        found.append((stride, members))
        stride *= members
    return found


def tree_sum(parts):
    while len(parts) > 1:
        parts = [first + second for first, second in zip(parts[::2], parts[1::2])]
    return parts[0]


def all_sum(value):
    for stride, members in stages(lax.axis_size("hid")):
        arrived = [flip(value, "hid", stride * k) for k in reversed(range(1, members))]
        value = tree_sum([value] + arrived[:1] + arrived[:0:-1])
    return value


def gather_pieces(pieces, plan):
    pieces = dict(pieces)
    for stride, members in plan:
        for offset in list(pieces):
            for k in reversed(range(1, members)):
                pieces[offset ^ (stride * k)] = flip(pieces[offset], "hid", stride * k)
    return pieces


def body(section_inputs, w_in, w_out, warm_factor, pending_left, pending_right, incoming_left, incoming_right):
    w_in, w_out, inputs = w_in[0], w_out[0], section_inputs[0]
    ticks, rows_own, depth = inputs.shape
    hidden_units = w_out.shape[0]
    rank = warm_factor.shape[2]
    count, own = lax.axis_size("hid"), lax.axis_index("hid")
    rows = rows_own * count
    sections = lax.axis_size("pipe")
    full = 2 * rows * depth * hidden_units
    turned = lambda value: jnp.swapaxes(value, -1, -2)
    incoming = (turned(incoming_left), turned(incoming_right))
    warm = turned(warm_factor[0])
    wide = ((rows, hidden_units), BF16)
    left_form, right_form = ((rank, rows), F32), ((rank, depth), F32)
    chips = count // 2
    direct = stages(count) == [(1, 2), (2, chips)]

    plan = stages(count)
    by_rows = rows_own % 16 == 0
    if by_rows:
        rows_first, rows_later = on_device(
            begin_kernel,
            [(inputs.shape[1:], BF16), ((ticks - 1, rows_own, depth), BF16)],
            (inputs,),
            8 * full,
            "begin",
        )
        blocks = gather_pieces({0: rows_first}, plan[1:] + plan[:1])
        later = gather_pieces({0: rows_later}, plan[1:] + plan[:1])
        offsets, pieces, later = list(blocks), list(blocks.values()), list(later.values())
    else:
        everything = lax.all_gather(inputs, "hid", axis=1, tiled=True)
        offsets, pieces, later = [0], [everything[0]], [everything[1:]]
    block_form = ((rows, own_width(depth)), F32)
    warm_in = on_device(warm_kernel, ((2 * rank, hidden_units), BF16), (warm, w_in), full // 2, "warm")
    up, block, share = on_device(
        up_kernel,
        [wide, block_form, left_form],
        (*incoming, turned(pending_left[0]), turned(pending_right[0]), warm, w_out),
        full,
        "up",
        [pltpu.VMEM(*right_form)],
    )

    for tick in range(ticks):
        last = tick + 1 == ticks
        scratch = [pltpu.VMEM((rows, depth), BF16)]
        if tick == 0:
            hidden, proj = on_device(
                functools.partial(first_kernel, offsets),
                [wide, left_form],
                (*pieces, w_in, up, warm_in, share),
                full,
                "first",
                scratch,
            )
        else:
            warm_in = on_device(
                warm_kernel, ((2 * rank, hidden_units), BF16), (warm, w_in), full // 2, "warm"
            )
            mask = on_device(
                functools.partial(mask_kernel, offsets, tick - 1),
                wide,
                (*later, w_in, leaving),
                full,
                "mask",
                scratch,
            )
            hidden, proj, block = on_device(
                functools.partial(hidden_kernel, tick),
                [wide, left_form, block_form],
                (*incoming, both, warm, w_out, mask, warm_in),
                full,
                "hidden",
                [pltpu.VMEM(*right_form)],
            )
        merged = on_device(merged_kernel, ((rows, depth), F32), (block, hidden, w_in), full, "merged")
        if last and direct:
            outgoing = on_device(
                outgoing_kernel, ((chips, rows_own, depth), BF16), (merged,), full // 16, "outgoing"
            )
            arrived = flip(outgoing, "hid", 1)
        proj = all_sum(proj)
        partial_right = on_device(
            right_kernel, right_form, (proj, merged), full // 16, "right"
        )
        left_new, inverse = on_device(
            factor_kernel, [left_form, ((rank, rank), F32)], (proj,), full // 2, "factor"
        )
        if last and direct:
            packed = ((rows_own + 2 * rank, depth), BF16)
            own_rows, own_right, *packs = on_device(
                functools.partial(pack_kernel, chips),
                [((rows_own, depth), F32), right_form] + [packed] * (chips - 1),
                (merged, arrived, partial_right, flip(partial_right, "hid", 1)),
                full // 16,
                "pack",
            )
            packs = [flip(pack, "hid", 2 * k) for k, pack in reversed(list(enumerate(packs, 1)))][::-1]
            grads, warm = on_device(
                last_kernel,
                [((rows_own, depth), F32), right_form],
                (inverse, own_rows, own_right, *packs[-1:], *packs[:-1]),
                full // 16,
                "last",
            )
            break
        if last:
            grads = lax.psum_scatter(merged, "hid", scatter_dimension=0, tiled=True)
        warm, leaving = on_device(
            finish_kernel,
            [right_form, ((rank, rows + depth), F32)],
            (inverse, left_new, all_sum(partial_right)),
            full // 16,
            "finish",
        )
        if not last:
            both = lax.ppermute(leaving, "pipe", [(source, source - 1) for source in range(1, sections)])
    left_rows = lax.dynamic_slice_in_dim(left_new, own * rows_own, rows_own, 1)
    return grads[None], turned(left_rows)[None], turned(warm)[None]


def solution(mesh):
    placed = (
        P("pipe", None, "hid", None),
        P("pipe", None, "hid"),
        P("pipe", "hid", None),
        P("pipe", None, None),
        P("pipe", None, None),
        P("pipe", None, None),
        P(),
        P(),
    )
    return jax.shard_map(
        body,
        mesh=mesh,
        in_specs=placed,
        out_specs=(P("pipe", "hid", None), P("pipe", "hid", None), P("pipe", None, None)),
        check_vma=False,
    )
```

```python
import functools

import jax
import jax.numpy as jnp
from jax import lax
from jax.experimental import pallas as pl
from jax.experimental.pallas import tpu as pltpu
from jax.sharding import PartitionSpec as P

F32 = jnp.float32
BF16 = jnp.bfloat16
HIGH = lax.Precision.HIGHEST
VMEM = pl.BlockSpec(memory_space=pltpu.VMEM)
HBM = pl.BlockSpec(memory_space=pltpu.HBM)
MIB = 1 << 20


def dot(first, second, first_dim, second_dim, precision=None):
    return lax.dot_general(
        first,
        second,
        (((first_dim,), (second_dim,)), ((), ())),
        precision=precision,
        preferred_element_type=F32,
    )


def split(value):
    high = value.astype(BF16)
    low = (value - high.astype(F32)).astype(BF16)
    return jnp.concatenate([high, low], 0)


def chunks(total, most=512):
    size = min(total, most)
    return [(start, size) for start in range(0, total, size)]


def left_parts(left_t):
    left = left_t.T
    high = left.astype(BF16)
    low = (left - high.astype(F32)).astype(BF16)
    return jnp.concatenate([high, high, low], 1)


def right_parts(right_t):
    high = right_t.astype(BF16)
    low = (right_t - high.astype(F32)).astype(BF16)
    return jnp.concatenate([high, low, high], 0)


def cotangent_of(lefts, right_t):
    return dot(lefts, right_parts(right_t), 1, 0)


def chosen(incoming, other):
    return jnp.where(lax.axis_index("pipe") == lax.axis_size("pipe") - 1, incoming, other)


def own_columns(depth):
    share = depth // lax.axis_size("hid")
    if share % 128 == 0:
        return pl.ds(pl.multiple_of(lax.axis_index("hid") * share, share), share), 1.0
    return slice(0, depth), jnp.where(lax.axis_index("hid") == 0, 1.0, 0.0)


def own_width(depth):
    share = depth // lax.axis_size("hid")
    return share if share % 128 == 0 else depth


def on_device(kernel, outs, operands, flops, name, scratch=(), far=0, limit=8):
    many = isinstance(outs, list)
    shapes = [jax.ShapeDtypeStruct(*out) for out in (outs if many else [outs])]
    result = pl.pallas_call(
        kernel,
        out_shape=shapes,
        in_specs=[VMEM] * (len(operands) - far) + [HBM] * far,
        out_specs=[VMEM] * len(shapes),
        scratch_shapes=list(scratch),
        compiler_params=pltpu.CompilerParams(vmem_limit_bytes=limit * MIB),
        cost_estimate=pl.CostEstimate(flops=flops, bytes_accessed=1 << 20, transcendentals=0),
        name=name,
    )(*operands)
    return result if many else result[0]


def begin_kernel(rows_ref, first_ref, later_ref):
    first_ref[...] = rows_ref[0]
    later_ref[...] = rows_ref[1:]


def up_kernel(in_left, in_right, pend_left, pend_right, warm_ref, w_out_ref, up_ref, block_ref, proj_ref, right_ref):
    left = chosen(in_left[0], pend_left[...])
    right_ref[...] = chosen(in_right[0], pend_right[...])
    lefts = left_parts(left)
    own_share(lefts, right_ref, warm_ref, block_ref, proj_ref)
    cotangent_low = cotangent_of(lefts, right_ref[...]).astype(BF16)
    for start, size in chunks(w_out_ref.shape[0]):
        up_ref[:, start : start + size] = dot(cotangent_low, w_out_ref[start : start + size, :], 1, 1).astype(BF16)


def own_share(lefts, right_ref, warm_ref, block_ref, proj_ref):
    here, factor = own_columns(right_ref.shape[1])
    block = cotangent_of(lefts, right_ref[:, here]) * factor
    block_ref[...] = block
    high = block.astype(BF16)
    low = (block - high.astype(F32)).astype(BF16)
    warm = split(warm_ref[:, here])
    proj_ref[...] = jnp.zeros_like(proj_ref)
    add_projected(dot(high, warm, 1, 1) + dot(low, warm, 1, 1), proj_ref)


def warm_into(stacked, w_in_ref, out_ref, start, size):
    rank = stacked.shape[0] // 2
    both = dot(stacked, w_in_ref[:, start : start + size], 1, 0)
    out_ref[:, start : start + size] = split(both[:rank] + both[rank:])


def warm_kernel(warm_ref, w_in_ref, out_ref):
    stacked = split(warm_ref[...])
    for start, size in chunks(w_in_ref.shape[1]):
        warm_into(stacked, w_in_ref, out_ref, start, size)


def place_rows(offsets, pieces, rows_ref):
    block = pieces[0].shape[0]
    for offset, piece in zip(offsets, pieces):
        place = 0
        if len(pieces) > 1:
            place = pl.multiple_of(jnp.bitwise_xor(lax.axis_index("hid"), offset) * block, block)
        rows_ref[pl.ds(place, block), :] = piece[...]


def project(hidden, warm_in_ref, start, size, total):
    part = dot(hidden, warm_in_ref[:, start : start + size], 1, 1)
    return part if total is None else total + part


def add_projected(total, proj_ref):
    rank = proj_ref.shape[0]
    turned = total.T
    proj_ref[...] += turned[:rank] + turned[rank:]


def first_kernel(offsets, *refs):
    pieces, rest = refs[: len(offsets)], refs[len(offsets) :]
    w_in_ref, up_ref, warm_in_ref, share_ref, hidden_ref, proj_ref, rows_ref = rest
    place_rows(offsets, pieces, rows_ref)
    total = None
    for start, size in chunks(w_in_ref.shape[1]):
        preact = dot(rows_ref[...], w_in_ref[:, start : start + size], 1, 0)
        hidden = jnp.where(preact > 0, up_ref[:, start : start + size].astype(F32), 0.0).astype(BF16)
        hidden_ref[:, start : start + size] = hidden
        total = project(hidden, warm_in_ref, start, size, total)
    proj_ref[...] = share_ref[...]
    add_projected(total, proj_ref)


def mask_kernel(offsets, step, *refs):
    pieces, (w_in_ref, _, mask_ref, rows_ref) = refs[: len(offsets)], refs[len(offsets) :]
    place_rows(offsets, [piece.at[step] for piece in pieces], rows_ref)
    for start, size in chunks(w_in_ref.shape[1]):
        preact = dot(rows_ref[...], w_in_ref[:, start : start + size], 1, 0)
        mask_ref[:, start : start + size] = jnp.where(preact > 0, 1.0, 0.0).astype(BF16)


def hidden_kernel(
    tick, in_left_ref, in_right_ref, both_ref, warm_ref, w_out_ref, mask_ref, warm_in_ref,
    hidden_ref, proj_ref, block_ref, right_ref,
):
    rows = hidden_ref.shape[0]
    lefts = left_parts(chosen(in_left_ref[tick], both_ref[:, :rows]))
    right_ref[...] = chosen(in_right_ref[tick], both_ref[:, rows:])
    cotangent_low = cotangent_of(lefts, right_ref[...]).astype(BF16)
    own_share(lefts, right_ref, warm_ref, block_ref, proj_ref)
    total = None
    for start, size in chunks(w_out_ref.shape[0]):
        up = dot(cotangent_low, w_out_ref[start : start + size, :], 1, 1)
        mask = mask_ref[:, start : start + size]
        hidden = jnp.where(mask.astype(F32) > 0, up, 0.0).astype(BF16)
        hidden_ref[:, start : start + size] = hidden
        total = project(hidden, warm_in_ref, start, size, total)
    add_projected(total, proj_ref)


def merged_kernel(block_ref, hidden_ref, w_in_ref, merged_ref):
    depth = w_in_ref.shape[0]
    size = min(depth, 256)
    for start in range(0, depth, size):
        here = slice(start, start + size)
        merged_ref[:, here] = dot(hidden_ref[...], w_in_ref[here, :], 1, 1)
    here, _ = own_columns(depth)
    merged_ref[:, here] += block_ref[...]


def right_kernel(proj_ref, merged_ref, out_ref):
    stacked = split(proj_ref[...])
    rank = proj_ref.shape[0]
    merged = merged_ref[...]
    high = merged.astype(BF16)
    low = (merged - high.astype(F32)).astype(BF16)
    both = dot(stacked, high, 1, 0) + dot(stacked, low, 1, 0)
    out_ref[...] = both[:rank] + both[rank:]


def factor_kernel(proj_ref, left_ref, inverse_ref):
    proj = proj_ref[...]
    rank = proj.shape[0]
    gram = dot(proj, proj, 1, 1, HIGH)
    line = lax.broadcasted_iota(jnp.int32, (rank, rank), 0)
    column = lax.broadcasted_iota(jnp.int32, (rank, rank), 1)
    eye = jnp.where(line == column, 1.0, 0.0)
    inverse = eye
    for step in range(rank):
        pivot_row = gram[step : step + 1, :]
        pivot = gram[step : step + 1, step : step + 1]
        scale = jnp.where(line[:, :1] > step, gram[:, step : step + 1] / pivot, 0.0)
        inverse = inverse - scale * inverse[step : step + 1, :]
        gram = gram - scale * pivot_row
    pivots = jnp.sum(gram * eye, axis=1, keepdims=True)
    inverse = inverse * lax.rsqrt(pivots)
    inverse_ref[...] = inverse
    left_ref[...] = dot(inverse, proj, 1, 0, HIGH)


def finish_kernel(inverse_ref, left_ref, sums_ref, right_ref, both_ref):
    right = dot(inverse_ref[...], sums_ref[...], 1, 0, HIGH)
    rows = left_ref.shape[1]
    right_ref[...] = right
    both_ref[:, :rows] = left_ref[...]
    both_ref[:, rows:] = right


def outgoing_kernel(merged_ref, out_ref):
    block = out_ref.shape[1]
    for chip in range(out_ref.shape[0]):
        start = pl.multiple_of((2 * chip + 1 - lax.axis_index("hid") % 2) * block, block)
        out_ref[chip] = merged_ref[pl.ds(start, block), :].astype(BF16)


def pack_kernel(chips, merged_ref, arrived_ref, right_ref, right_arrived_ref, own_ref, right_out, *out_refs):
    block = own_ref.shape[0]
    core, chip = lax.axis_index("hid") % 2, lax.axis_index("hid") // 2
    stacked = split(right_ref[...] + right_arrived_ref[...])
    rank = right_ref.shape[0]
    right_out[...] = stacked[:rank].astype(F32) + stacked[rank:].astype(F32)
    for turn in range(chips):
        target = jnp.bitwise_xor(chip, turn)
        start = pl.multiple_of((2 * target + core) * block, block)
        value = merged_ref[pl.ds(start, block), :] + arrived_ref[target].astype(F32)
        if turn:
            out_refs[turn - 1][:block, :] = value.astype(BF16)
            out_refs[turn - 1][block:, :] = stacked
        else:
            own_ref[...] = value


def last_kernel(inverse_ref, own_ref, right_own_ref, *refs):
    packs, (grads_ref, right_ref) = refs[:-2], refs[-2:]
    block, rank = own_ref.shape[0], inverse_ref.shape[0]
    rows = [own_ref[...]] + [pack[:block, :].astype(F32) for pack in packs]
    sums = [right_own_ref[...]] + [
        pack[block : block + rank, :].astype(F32) + pack[block + rank :, :].astype(F32) for pack in packs
    ]
    grads_ref[...] = tree_sum(rows)
    right_ref[...] = dot(inverse_ref[...], tree_sum(sums), 1, 0, HIGH)


def flip(value, axis, bits):
    count = lax.axis_size(axis)
    return lax.ppermute(value, axis, [(source, source ^ bits) for source in range(count)])


def stages(count):
    found, stride = [], 1
    while stride < count:
        members = 2 if stride == 1 else min(4, count // stride)
        found.append((stride, members))
        stride *= members
    return found


def tree_sum(parts):
    while len(parts) > 1:
        parts = [first + second for first, second in zip(parts[::2], parts[1::2])]
    return parts[0]


def all_sum(value):
    for stride, members in stages(lax.axis_size("hid")):
        arrived = [flip(value, "hid", stride * k) for k in reversed(range(1, members))]
        value = tree_sum([value] + arrived[:1] + arrived[:0:-1])
    return value


def gather_pieces(pieces, plan, order=reversed):
    pieces = dict(pieces)
    for stride, members in plan:
        for offset in list(pieces):
            for k in order(range(1, members)):
                pieces[offset ^ (stride * k)] = flip(pieces[offset], "hid", stride * k)
    return pieces


def body(section_inputs, w_in, w_out, warm_factor, pending_left, pending_right, incoming_left, incoming_right):
    w_in, w_out, inputs = w_in[0], w_out[0], section_inputs[0]
    ticks, rows_own, depth = inputs.shape
    hidden_units = w_out.shape[0]
    rank = warm_factor.shape[2]
    count, own = lax.axis_size("hid"), lax.axis_index("hid")
    rows = rows_own * count
    sections = lax.axis_size("pipe")
    full = 2 * rows * depth * hidden_units
    turned = lambda value: jnp.swapaxes(value, -1, -2)
    incoming = (turned(incoming_left), turned(incoming_right))
    warm = turned(warm_factor[0])
    wide = ((rows, hidden_units), BF16)
    left_form, right_form = ((rank, rows), F32), ((rank, depth), F32)
    chips = count // 2
    direct = stages(count) == [(1, 2), (2, chips)]

    plan = stages(count)
    by_rows = rows_own % 16 == 0
    if by_rows:
        rows_first, rows_later = on_device(
            begin_kernel,
            [(inputs.shape[1:], BF16), ((ticks - 1, rows_own, depth), BF16)],
            (inputs,),
            8 * full,
            "begin",
        )
        blocks = gather_pieces({0: rows_first}, plan[1:] + plan[:1])
        later = gather_pieces({0: rows_later}, plan[1:] + plan[:1], list)
        offsets, pieces, later = list(blocks), list(blocks.values()), [later[offset] for offset in blocks]
    else:
        everything = lax.all_gather(inputs, "hid", axis=1, tiled=True)
        offsets, pieces, later = [0], [everything[0]], [everything[1:]]
    block_form = ((rows, own_width(depth)), F32)
    warm_in = on_device(warm_kernel, ((2 * rank, hidden_units), BF16), (warm, w_in), full // 2, "warm")
    up, block, share = on_device(
        up_kernel,
        [wide, block_form, left_form],
        (*incoming, turned(pending_left[0]), turned(pending_right[0]), warm, w_out),
        full,
        "up",
        [pltpu.VMEM(*right_form)],
    )

    for tick in range(ticks):
        last = tick + 1 == ticks
        scratch = [pltpu.VMEM((rows, depth), BF16)]
        if tick == 0:
            hidden, proj = on_device(
                functools.partial(first_kernel, offsets),
                [wide, left_form],
                (*pieces, w_in, up, warm_in, share),
                full,
                "first",
                scratch,
            )
        else:
            warm_in = on_device(
                warm_kernel, ((2 * rank, hidden_units), BF16), (warm, w_in), full // 2, "warm"
            )
            mask = on_device(
                functools.partial(mask_kernel, offsets, tick - 1),
                wide,
                (*later, w_in, leaving),
                full,
                "mask",
                scratch,
            )
            hidden, proj, block = on_device(
                functools.partial(hidden_kernel, tick),
                [wide, left_form, block_form],
                (*incoming, both, warm, w_out, mask, warm_in),
                full,
                "hidden",
                [pltpu.VMEM(*right_form)],
            )
        merged = on_device(merged_kernel, ((rows, depth), F32), (block, hidden, w_in), full, "merged")
        if last and direct:
            outgoing = on_device(
                outgoing_kernel, ((chips, rows_own, depth), BF16), (merged,), full // 16, "outgoing"
            )
            arrived = flip(outgoing, "hid", 1)
        proj = all_sum(proj)
        partial_right = on_device(
            right_kernel, right_form, (proj, merged), full // 16, "right"
        )
        left_new, inverse = on_device(
            factor_kernel, [left_form, ((rank, rank), F32)], (proj,), full // 2, "factor"
        )
        if last and direct:
            packed = ((rows_own + 2 * rank, depth), BF16)
            own_rows, own_right, *packs = on_device(
                functools.partial(pack_kernel, chips),
                [((rows_own, depth), F32), right_form] + [packed] * (chips - 1),
                (merged, arrived, partial_right, flip(partial_right, "hid", 1)),
                full // 16,
                "pack",
            )
            packs = [flip(pack, "hid", 2 * k) for k, pack in reversed(list(enumerate(packs, 1)))][::-1]
            grads, warm = on_device(
                last_kernel,
                [((rows_own, depth), F32), right_form],
                (inverse, own_rows, own_right, *packs[-1:], *packs[:-1]),
                full // 16,
                "last",
            )
            break
        if last:
            grads = lax.psum_scatter(merged, "hid", scatter_dimension=0, tiled=True)
        warm, leaving = on_device(
            finish_kernel,
            [right_form, ((rank, rows + depth), F32)],
            (inverse, left_new, all_sum(partial_right)),
            full // 16,
            "finish",
        )
        if not last:
            both = lax.ppermute(leaving, "pipe", [(source, source - 1) for source in range(1, sections)])
    left_rows = lax.dynamic_slice_in_dim(left_new, own * rows_own, rows_own, 1)
    return grads[None], turned(left_rows)[None], turned(warm)[None]


def solution(mesh):
    placed = (
        P("pipe", None, "hid", None),
        P("pipe", None, "hid"),
        P("pipe", "hid", None),
        P("pipe", None, None),
        P("pipe", None, None),
        P("pipe", None, None),
        P(),
        P(),
    )
    return jax.shard_map(
        body,
        mesh=mesh,
        in_specs=placed,
        out_specs=(P("pipe", "hid", None), P("pipe", "hid", None), P("pipe", None, None)),
        check_vma=False,
    )
```
